256 devices in a mesh: dp: 4 (over y), vocab: 64 (over x, z, core).
Axes of the slice: x: 4, y: 4, z: 8, core: 2. Of those that a mesh axis runs over, the one named last changes fastest.
Arguments:
- hidden: bfloat16 [4096, 2304], P(('dp', 'vocab')), parts along dimension 0, may hold values from -6 to 6
- norm_gain: float32 [2304], replicated, may hold values from 0.1 to 1.9
- head_weight: bfloat16 [2304, 131072], P(None, 'vocab'), may hold values from -1.875 to 1.875
Outputs:
- log_probs: bfloat16 [4096, 131072], P(('dp', 'vocab')), parts along dimension 0
The draws below stay inside these ranges and needn't reach their ends.
There are 4 independent parts, one for each index of `dp`. The reference program is written for one: setup_inputs(seed, part) draws one part's arguments, and reference() takes and returns one part's arrays. A program takes and returns all parts, laid end to end along the dimension named above; an argument that names none is the same for every part. Nothing has to cross between parts.
All inputs are finite; a program needn't handle non-finite values.
Results may differ from the reference program's by a relative error of at most 0.0025.
Values may be sent and summed in bfloat16 or wider, within the bound.
A program may use at most 64 MiB of HBM per device.

```python
import math
import jax
import jax.numpy as jnp
from jax import lax

D = 2304
ROWS = 1024
VOCAB = 131072


def draw_head_weight(key, part):
    key = jax.random.fold_in(key, 7)
    first, second = jax.random.split(key)
    ramp = 1.0 + 2.0 * jnp.arange(VOCAB, dtype=jnp.float32) / VOCAB
    base = jnp.clip(jax.random.normal(first, (D, VOCAB), jnp.float32), -3.0, 3.0)
    spread = jnp.exp(jax.random.uniform(second, (VOCAB,), jnp.float32, 0.0, math.log(10.0)))
    return (base * (spread * ramp)[None, :] / math.sqrt(D)).astype(jnp.bfloat16)


def block_levels(own_key, extent, shards, least, largest):
    loudness = 1.0
    for axis_at, shards_of in shards:
        steps = jax.random.uniform(jax.random.fold_in(jax.random.fold_in(own_key, 6), axis_at), (shards_of,), jnp.float32, least / len(shards), largest / len(shards))
        loudness = loudness * jnp.repeat(jnp.exp(steps), extent[axis_at] // shards_of).reshape((-1,) + (1,) * (len(extent) - 1 - axis_at))
    return loudness


def normal_values(stream_key, shape, width, reach, shards=(), kind=jnp.bfloat16):
    values = width * jax.random.normal(stream_key, shape, jnp.float32)
    if shards:
        values = values * block_levels(stream_key, shape, shards, -0.22, 0.18)
    return jnp.clip(values, -reach, reach).astype(kind)


def setup_inputs(seed: int = 0, part: int = 0) -> dict:
    key_list = jax.random.split(jax.random.key(seed), 4)
    part_keys = jax.random.split(jax.random.fold_in(key_list[3], part), 4)
    hidden = normal_values(part_keys[0], (ROWS, D), 1.0, 6.0, ((0, 64),))
    norm_gain = jnp.clip(1.0 + 0.18 * jax.random.normal(key_list[1], (D,), jnp.float32), 0.1, 1.9)
    head_weight = draw_head_weight(jax.random.fold_in(key_list[3], 71), part)
    return dict(hidden=hidden, norm_gain=norm_gain, head_weight=head_weight)


def reference(hidden, norm_gain, head_weight):
    values = hidden.astype(jnp.float32)
    power = lax.optimization_barrier(jnp.mean(values * values, axis=1, keepdims=True))
    normed = (values * jax.lax.rsqrt(power + 1e-06) * norm_gain[None, :]).astype(jnp.bfloat16)
    logits = jnp.dot(normed, head_weight, preferred_element_type=jnp.float32)
    scaled = 15.0 * jnp.tanh(logits / 30.0)
    total = lax.optimization_barrier(jnp.sum(jnp.exp(scaled - 15.0), axis=1, keepdims=True))
    return (scaled - 15.0 - jnp.log(total)).astype(jnp.bfloat16)
```

```python
import functools
import math

import jax
import jax.numpy as jnp
from jax import lax
from jax.experimental import pallas as pl
from jax.experimental.pallas import tpu as pltpu
from jax.sharding import PartitionSpec as P

X, Z, C = 4, 8, 2
N = X * Z * C
ROWS = 16
CODE = 5.5
MESH = pl.DeviceIdType.MESH
TILE = 512


def depths(q):
    return (0, 4) if q == 3 else (q + 1, 7 - q)


def make_slots():
    table = []
    for q in range(4):
        for dc in range(2):
            table += [(0, dz, dc) for dz in depths(q)]
    for q in range(4):
        for dc in range(2):
            table += [(dx, dz, dc) for dx in (1, 3) for dz in depths(q)]
    for q in range(4):
        for dc in range(2):
            table += [(2, dz, dc) for dz in depths(q)]
    return table


SLOTS = make_slots()
SLOT = {place: i for i, place in enumerate(SLOTS)}
CHUNKS = [(4 * q, 4) for q in range(4)] + [(16 + 8 * q, 8) for q in range(6)]


def kernel(hidden, gain, head, coded, shift, w, g, sbuf, rbuf, acc, w_sem, out_sem, gs_sem, gr_sem, os_sem, or_sem):
    v = lax.axis_index("vocab")
    y = lax.axis_index("dp")
    x, z, c = v // (Z * C), (v // C) % Z, v % C

    def at(dx, dz, dc):
        return (y, (((x + dx) % X) * Z + (z + dz) % Z) * C + (c + dc) % C)

    barrier = pltpu.get_barrier_semaphore()

    def greet(i, carry):
        pl.semaphore_signal(barrier, inc=1, device_id=(y, (v + i) % N), device_id_type=MESH)
        return carry

    lax.fori_loop(1, N, greet, 0)
    loads = []
    for n in range(2048 // TILE):
        cols = pl.ds(n * TILE, TILE)
        loads.append(pltpu.make_async_copy(head.at[:, cols], w.at[:, cols], w_sem.at[n]))
        loads[-1].start()

    wide = hidden[...].astype(jnp.float32)
    power = jnp.mean(wide * wide, axis=1, keepdims=True)
    own = SLOT[0, 0, 0]
    g[own] = (wide * lax.rsqrt(power + 1e-06) * gain[...]).astype(jnp.bfloat16)
    acc[...] = jnp.zeros_like(acc)
    pl.semaphore_wait(barrier, N - 1)

    sends = []
    arrivals = {}

    def push(place, count, step, cols=None):
        dx, dz, dc = place
        ex, ez, ec = step
        to = SLOT[(dx - ex) % X, (dz - ez) % Z, (dc + ec) % 2]
        src, dst = g.at[pl.ds(SLOT[place], count)], g.at[pl.ds(to, count)]
        if cols is not None:
            src, dst = src.at[:, :, cols], dst.at[:, :, cols]
        k = len(sends)
        copy = pltpu.make_async_remote_copy(
            src_ref=src, dst_ref=dst, send_sem=gs_sem.at[k], recv_sem=gr_sem.at[k],
            device_id=at(ex, ez, ec), device_id_type=MESH,
        )
        copy.start()
        sends.append(copy)
        return copy

    halves = (pl.ds(0, 1152), pl.ds(1152, 1152))
    sideways = ((1, 0, 0), (3, 0, 0), (2, 0, 0))

    def spread(place, count):
        core = push(place, count, (0, 0, 1))
        rest = [push(place, count, step) for step in sideways]
        return core, rest

    down = push((0, 0, 0), 1, (0, 7, 0))
    up = push((0, 0, 0), 1, (0, 1, 0))
    core_own, side_own = spread((0, 0, 0), 1)
    x_in, core_in = {}, {}
    out_copies = []

    def compute(first, count):
        rows = count * ROWS

        def tile(n, carry):
            cols = pl.ds(pl.multiple_of(n * TILE, TILE), TILE)
            left = g[pl.ds(first, count)].reshape(rows, 2304)
            logits = jnp.dot(left, w[:, cols], preferred_element_type=jnp.float32)
            sent = jnp.exp((15.0 * CODE) * jnp.tanh(logits * (1.0 / 30.0))).astype(jnp.bfloat16)
            sbuf[pl.ds(first, count), :, cols] = sent.reshape(count, ROWS, TILE)
            return carry

        lax.fori_loop(0, 2048 // TILE, tile, 0)
        for s in range(first, first + count):
            dx, dz, dc = SLOTS[s]
            if s == own:
                continue
            to = SLOT[(-dx) % X, (-dz) % Z, dc]
            copy = pltpu.make_async_remote_copy(
                src_ref=sbuf.at[s], dst_ref=rbuf.at[to], send_sem=os_sem.at[s], recv_sem=or_sem.at[to],
                device_id=at(dx, dz, dc), device_id_type=MESH,
            )
            copy.start()
            out_copies.append(copy)

    for q in range(4):
        k = q + 1
        if q < 3:
            down.wait_recv()
            up.wait_recv()
            if k < 3:
                down = push((0, k, 0), 1, (0, 7, 0))
                up = push((0, 8 - k, 0), 1, (0, 1, 0))
            else:
                down = push((0, 3, 0), 1, (0, 7, 0), halves[0])
                up = push((0, 5, 0), 1, (0, 1, 0), halves[1])
            core_in[q], x_in[q] = spread((0, k, 0), 2)
            core_in[q].wait_recv()
        else:
            down.wait_recv()
            up.wait_recv()
            core_in[q], x_in[q] = spread((0, 4, 0), 1)
            core_own.wait_recv()
            core_in[q].wait_recv()
        if q == 0:
            for load in loads:
                load.wait()
        compute(*CHUNKS[q])

    for q in range(4):
        sources = x_in[q][:2] + (side_own[:2] if q == 3 else [])
        for copy in sources:
            copy.wait_recv()
        swap = push((1, depths(q)[0], 0), 4, (0, 0, 1))
        swap.wait_recv()
        compute(*CHUNKS[4 + q])
    for half in range(2):
        for q in (2 * half, 2 * half + 1):
            x_in[q][2].wait_recv()
            if q == 3:
                side_own[2].wait_recv()
        swaps = [push((2, depths(q)[0], 0), 2, (0, 0, 1)) for q in (2 * half, 2 * half + 1)]
        for swap in swaps:
            swap.wait_recv()
        compute(*CHUNKS[8 + half])

    log2e = 1.0 / math.log(2.0)

    def take(s):
        dx, dz, dc = SLOTS[s]
        buf = sbuf if s == own else rbuf
        column = at(dx, dz, dc)[1] * 2048
        store = pltpu.make_async_copy(
            buf.at[s], coded.at[:, pl.ds(pl.multiple_of(column, 2048), 2048)], out_sem.at[s]
        )
        store.start()
        total = acc[...]
        for n in range(0, 2048, TILE):
            part = jnp.exp(jnp.log(buf[s, :, n : n + TILE].astype(jnp.float32)) * (1.0 / CODE) - 15.0)
            for m in range(0, TILE, 128):
                total += part[:, m : m + 128]
        acc[...] = total
        return store

    stores = [take(own)]
    for s in range(N):
        if s == own:
            continue
        dx, dz, dc = SLOTS[s]
        pltpu.make_async_remote_copy(
            src_ref=sbuf.at[s], dst_ref=rbuf.at[s], send_sem=os_sem.at[s], recv_sem=or_sem.at[s],
            device_id=at(dx, dz, dc), device_id_type=MESH,
        ).wait_recv()
        stores.append(take(s))
    total = jnp.sum(acc[...], axis=1, keepdims=True)
    shift[...] = jnp.broadcast_to(15.0 + jnp.log(total), shift.shape)
    for copy in sends:
        copy.wait_send()
    for copy in out_copies:
        copy.wait_send()
    for store in stores:
        store.wait()


def local(hidden, norm_gain, head_weight):
    vmem = pl.BlockSpec(memory_space=pltpu.VMEM)
    hbm = pl.BlockSpec(memory_space=pl.ANY)
    coded, shift = pl.pallas_call(
        kernel,
        name="gather_head_exchange",
        out_shape=(
            jax.ShapeDtypeStruct((ROWS, N * 2048), jnp.bfloat16),
            jax.ShapeDtypeStruct((ROWS, 128), jnp.float32),
        ),
        in_specs=[vmem, vmem, hbm],
        out_specs=(hbm, vmem),
        scratch_shapes=[
            pltpu.VMEM((2304, 2048), jnp.bfloat16),
            pltpu.VMEM((N, ROWS, 2304), jnp.bfloat16),
            pltpu.VMEM((N, ROWS, 2048), jnp.bfloat16),
            pltpu.VMEM((N, ROWS, 2048), jnp.bfloat16),
            pltpu.VMEM((ROWS, 128), jnp.float32),
            pltpu.SemaphoreType.DMA((2048 // TILE,)),
            pltpu.SemaphoreType.DMA((N,)),
            pltpu.SemaphoreType.DMA((N,)),
            pltpu.SemaphoreType.DMA((N,)),
            pltpu.SemaphoreType.DMA((N,)),
            pltpu.SemaphoreType.DMA((N,)),
        ],
        compiler_params=pltpu.CompilerParams(
            collective_id=0, has_side_effects=True, vmem_limit_bytes=40 * 1024 * 1024
        ),
        cost_estimate=pl.CostEstimate(
            flops=2 * N * ROWS * 2304 * 2048, bytes_accessed=18 * 1024 * 1024, transcendentals=4 * N * ROWS * 2048
        ),
    )(hidden, norm_gain[None, :], head_weight)
    scaled = jnp.log(coded.astype(jnp.float32)) * (1.0 / CODE)
    return (scaled - shift[:, :1]).astype(jnp.bfloat16)


def solution(mesh):
    in_specs = (P(("dp", "vocab"), None), P(), P(None, "vocab"))
    out_specs = P(("dp", "vocab"), None)
    return jax.shard_map(local, mesh=mesh, in_specs=in_specs, out_specs=out_specs, check_vma=False)
```

```python
import jax
import jax.numpy as jnp
from jax import lax
from jax.experimental import pallas as pl
from jax.experimental.pallas import tpu as pltpu
from jax.sharding import PartitionSpec as P

X, Z, C = 4, 8, 2
N = X * Z * C
ROWS = 16
D = 2304
OWN = 2048
CODE = 5.5
MESH = pl.DeviceIdType.MESH
TILE = 1024
DEPTHS = (1, 7, 2, 6, 3, 5, 0, 4)
MIXED = (1, 7, 4, 2, 6, 3, 5, 0)


def make_slots():
    table = [(0, dz, dc) for q in range(4) for dc in range(2) for dz in DEPTHS[2 * q : 2 * q + 2]]
    for dx in (1, 3, 2):
        table += [(dx, dz, dc) for dc in range(2) for dz in DEPTHS]
    return table


SLOTS = make_slots()
SLOT = {place: i for i, place in enumerate(SLOTS)}
SELF = SLOT[0, 0, 0]


def kernel(hidden, gain, head, scaled, shift, h, gn, w, g, sbuf, rbuf, acc, in_sem, w_sem, gs_sem, gr_sem, os_sem, or_sem):
    v = lax.axis_index("vocab")
    y = lax.axis_index("dp")
    x, z, c = v // (Z * C), (v // C) % Z, v % C

    def index(dx, dz, dc):
        return (((x + dx) % X) * Z + (z + dz) % Z) * C + (c + dc) % C

    def at(dx, dz, dc):
        return (y, index(dx, dz, dc))

    barrier = pltpu.get_barrier_semaphore()
    partners = ((0, 1, 0), (0, 7, 0), (1, 0, 0), (3, 0, 0), (2, 0, 0), (0, 0, 1))
    for step in partners:
        pl.semaphore_signal(barrier, inc=1, device_id=at(*step), device_id_type=MESH)

    inputs = [pltpu.make_async_copy(hidden, h, in_sem.at[0]), pltpu.make_async_copy(gain, gn, in_sem.at[1])]
    for copy in inputs:
        copy.start()
    loads = []
    for n in range(OWN // TILE):
        cols = pl.ds(n * TILE, TILE)
        loads.append(pltpu.make_async_copy(head.at[:, cols], w.at[:, cols], w_sem.at[n]))
        loads[-1].start()
    for copy in inputs:
        copy.wait()
    wide = h[...].astype(jnp.float32)
    power = jnp.mean(wide * wide, axis=1, keepdims=True)
    g[SELF] = (wide * lax.rsqrt(power + 1e-06) * gn[...].reshape(1, D)).astype(jnp.bfloat16)
    acc[...] = jnp.zeros_like(acc)
    pl.semaphore_wait(barrier, len(partners))

    sends = []

    def push(place, count, step, cols=None):
        dx, dz, dc = place
        ex, ez, ec = step
        to = SLOT[(dx - ex) % X, (dz - ez) % Z, (dc + ec) % C]
        src, dst = g.at[pl.ds(SLOT[place], count)], g.at[pl.ds(to, count)]
        if cols is not None:
            src, dst = src.at[:, :, cols], dst.at[:, :, cols]
        k = len(sends)
        copy = pltpu.make_async_remote_copy(
            src_ref=src, dst_ref=dst, send_sem=gs_sem.at[k], recv_sem=gr_sem.at[k],
            device_id=at(*step), device_id_type=MESH,
        )
        copy.start()
        sends.append(copy)
        return copy

    from_x = {1: [], 3: [], 2: []}

    def spread(place, count):
        swap = push(place, count, (0, 0, 1))
        for dx in (1, 3, 2):
            from_x[dx].append(push(place, count, ((-dx) % X, 0, 0)))
        return swap

    def multiply(first, count):
        def tile(n, carry):
            cols = pl.ds(pl.multiple_of(n * TILE, TILE), TILE)
            left = g[pl.ds(first, count)].reshape(count * ROWS, D)
            logits = jnp.dot(left, w[:, cols], preferred_element_type=jnp.float32)
            sent = jnp.exp((15.0 * CODE) * jnp.tanh(logits * (1.0 / 30.0))).astype(jnp.bfloat16)
            sbuf[pl.ds(first, count), :, cols] = sent.reshape(count, ROWS, TILE)
            return carry

        lax.fori_loop(0, OWN // TILE, tile, 0)

    def result(s, to, step):
        return pltpu.make_async_remote_copy(
            src_ref=sbuf.at[s], dst_ref=rbuf.at[to], send_sem=os_sem.at[s], recv_sem=or_sem.at[to],
            device_id=at(*step), device_id_type=MESH,
        )

    results = []

    def compute(first, count):
        multiply(first, count)
        places = SLOTS[first : first + count]
        if count == 8:
            places = [(places[0][0], dz, places[0][2]) for dz in MIXED]
        for dx, dz, dc in places:
            if (dx, dz, dc) != (0, 0, 0):
                copy = result(SLOT[dx, dz, dc], SLOT[(-dx) % X, (-dz) % Z, dc], (dx, dz, dc))
                copy.start()
                results.append(copy)

    halves = (pl.ds(0, D // 2), pl.ds(D // 2, D // 2))
    down = push((0, 0, 0), 1, (0, 7, 0))
    up = push((0, 0, 0), 1, (0, 1, 0))
    swaps = [spread((0, 0, 0), 1)]
    for k in range(1, 4):
        down.wait_recv()
        up.wait_recv()
        last = k == 3
        down = push((0, k, 0), 1, (0, 7, 0), halves[0] if last else None)
        up = push((0, 8 - k, 0), 1, (0, 1, 0), halves[1] if last else None)
        swaps.append(spread((0, k, 0), 2))
        if k == 1:
            for load in loads:
                load.wait()
            compute(0, 2)
        else:
            swaps[k - 1].wait_recv()
            compute(4 * k - 6, 4)
    down.wait_recv()
    up.wait_recv()
    swaps.append(spread((0, 4, 0), 1))
    swaps[3].wait_recv()
    compute(10, 4)
    swaps[0].wait_recv()
    swaps[4].wait_recv()
    compute(14, 2)

    cross = {}
    for dx in (1, 3, 2):
        for copy in from_x[dx]:
            copy.wait_recv()
        cross[dx] = push((dx, 1, 0), 8, (0, 0, 1))
        compute(SLOT[dx, 1, 0], 8)
        if dx == 1:
            continue
        for late in (1, 3) if dx == 3 else (2,):
            cross[late].wait_recv()
            compute(SLOT[late, 1, 1], 8)

    def take(s, buf):
        column = index(*SLOTS[s]) * OWN
        total = acc[...]
        for n in range(0, OWN, 512):
            part = jnp.log(buf[s, :, n : n + 512].astype(jnp.float32)) * (1.0 / CODE)
            scaled[:, pl.ds(pl.multiple_of(column + n, 512), 512)] = part
            terms = jnp.exp(part - 15.0)
            for m in range(0, 512, 128):
                total += terms[:, m : m + 128]
        acc[...] = total

    take(SELF, sbuf)
    for s in range(N):
        if s != SELF:
            result(s, s, SLOTS[s]).wait_recv()
            take(s, rbuf)
    total = jnp.sum(acc[...], axis=1, keepdims=True)
    shift[...] = jnp.broadcast_to(15.0 + jnp.log(total), shift.shape)
    for copy in sends + results:
        copy.wait_send()


def local(hidden, norm_gain, head_weight):
    vmem = pl.BlockSpec(memory_space=pltpu.VMEM)
    anywhere = pl.BlockSpec(memory_space=pl.ANY)
    scaled, shift = pl.pallas_call(
        kernel,
        name="gather_head_exchange",
        out_shape=(
            jax.ShapeDtypeStruct((ROWS, N * OWN), jnp.float32),
            jax.ShapeDtypeStruct((ROWS, 128), jnp.float32),
        ),
        in_specs=[anywhere, anywhere, anywhere],
        out_specs=(vmem, vmem),
        scratch_shapes=[
            pltpu.VMEM((ROWS, D), jnp.bfloat16),
            pltpu.VMEM((D,), jnp.float32),
            pltpu.VMEM((D, OWN), jnp.bfloat16),
            pltpu.VMEM((N, ROWS, D), jnp.bfloat16),
            pltpu.VMEM((N, ROWS, OWN), jnp.bfloat16),
            pltpu.VMEM((N, ROWS, OWN), jnp.bfloat16),
            pltpu.VMEM((ROWS, 128), jnp.float32),
            pltpu.SemaphoreType.DMA((2,)),
            pltpu.SemaphoreType.DMA((OWN // TILE,)),
            pltpu.SemaphoreType.DMA((N,)),
            pltpu.SemaphoreType.DMA((N,)),
            pltpu.SemaphoreType.DMA((N,)),
            pltpu.SemaphoreType.DMA((N,)),
        ],
        compiler_params=pltpu.CompilerParams(
            collective_id=0, has_side_effects=True, vmem_limit_bytes=42 * 1024 * 1024
        ),
        cost_estimate=pl.CostEstimate(
            flops=2 * N * ROWS * D * OWN, bytes_accessed=18 * 1024 * 1024, transcendentals=4 * N * ROWS * OWN
        ),
    )(hidden, norm_gain, head_weight)
    return (scaled - shift[:, :1]).astype(jnp.bfloat16)


def solution(mesh):
    in_specs = (P(("dp", "vocab"), None), P(), P(None, "vocab"))
    out_specs = P(("dp", "vocab"), None)
    return jax.shard_map(local, mesh=mesh, in_specs=in_specs, out_specs=out_specs, check_vma=False)
```

```python
import jax
import jax.numpy as jnp
from jax import lax
from jax.experimental import pallas as pl
from jax.experimental.pallas import tpu as pltpu
from jax.sharding import PartitionSpec as P

X, Z, C = 4, 8, 2
N = X * Z * C
ROWS = 16
D = 2304
OWN = 2048
CODE = 5.5
MESH = pl.DeviceIdType.MESH
TILE = 1024
MIXED = (1, 7, 4, 2, 6, 3, 5, 0)


def near(k):
    return (k,) if k in (0, 4) else (k, Z - k)


def blocks(dxs, ks, dc):
    return [(dx, dz, dc) for k in ks for dx in dxs for dz in near(k)]


def plan():
    here, sides, far = (0,), (1, 3), (2,)
    steps = [("ring", blocks(here, (1,), 0)), ("product", blocks(here, (1,), 0))]
    steps += [("ring", blocks(here, (2,), 0)), ("product", blocks(here, (1,), 1) + blocks(here, (2,), 0))]
    steps += [("swap", blocks(sides, (0, 1), 0)), ("product", blocks(sides, (0, 1), 0))]
    steps += [("ring", blocks(here, (3,), 0)), ("product", blocks(here, (2,), 1) + blocks(here, (3,), 0))]
    steps += [("swap", blocks(sides, (2,), 0)), ("product", blocks(sides, (0, 1), 1) + blocks(sides, (2,), 0))]
    steps += [("ring", blocks(here, (4,), 0)), ("product", blocks(here, (3,), 1) + blocks(here, (0, 4), 0))]
    steps += [("swap", blocks(sides, (3,), 0)), ("product", blocks(sides, (2,), 1) + blocks(sides, (3,), 0))]
    steps += [("product", blocks(here, (0, 4), 1))]
    steps += [("swap", blocks(sides, (4,), 0)), ("product", blocks(sides, (3,), 1) + blocks(sides, (4,), 0))]
    every = (1, 2, 3, 0, 4)
    steps += [("swap", blocks(far, (0, 1, 2, 3, 4), 0)), ("product", blocks(sides, (4,), 1))]
    steps += [("last", blocks(far, (0, 1, 2, 3, 4), 0) + blocks(far, (0, 1, 2, 3, 4), 1))]
    return steps


LATE = [(0, 1), (1, 0), (2, 1), (5, 0), (6, 1), (3, 0), (4, 1), (7, 0), (0, 0), (1, 1), (2, 0), (5, 1), (6, 0), (3, 1), (4, 0), (7, 1)]
PIECES = {0: 4, 2: 2}
PLAN = plan()
SLOTS = [place for what, places in PLAN if what != "ring" and what != "swap" for place in places]
SLOT = {place: i for i, place in enumerate(SLOTS)}
SELF = SLOT[0, 0, 0]


def kernel(hidden, gain, head, scaled, shift, w, g, sbuf, rbuf, acc, w_sem, gs_sem, gr_sem, os_sem, or_sem):
    v = lax.axis_index("vocab")
    y = lax.axis_index("dp")
    x, z, c = v // (Z * C), (v // C) % Z, v % C

    def index(dx, dz, dc):
        return (((x + dx) % X) * Z + (z + dz) % Z) * C + (c + dc) % C

    def at(dx, dz, dc):
        return (y, index(dx, dz, dc))

    barrier = pltpu.get_barrier_semaphore()
    partners = ((0, 1, 0), (0, 7, 0), (1, 0, 0), (3, 0, 0), (2, 0, 0), (0, 0, 1))
    for step in partners:
        pl.semaphore_signal(barrier, inc=1, device_id=at(*step), device_id_type=MESH)

    loads = []
    for n in range(OWN // TILE):
        cols = pl.ds(n * TILE, TILE)
        loads.append(pltpu.make_async_copy(head.at[:, cols], w.at[:, cols], w_sem.at[n]))
        loads[-1].start()
    wide = hidden[...].astype(jnp.float32)
    power = jnp.mean(wide * wide, axis=1, keepdims=True)
    g[SELF] = (wide * lax.rsqrt(power + 1e-06) * gain[...].reshape(1, D)).astype(jnp.bfloat16)
    acc[...] = jnp.zeros_like(acc)
    pl.semaphore_wait(barrier, len(partners))

    sends = []

    def push(place, count, step, cols=None):
        dx, dz, dc = place
        ex, ez, ec = step
        to = SLOT[(dx - ex) % X, (dz - ez) % Z, (dc + ec) % C]
        for i in range(count):
            px, pz, pc = SLOTS[SLOT[place] + i]
            assert SLOTS[to + i] == ((px - ex) % X, (pz - ez) % Z, (pc + ec) % C)
        src, dst = g.at[pl.ds(SLOT[place], count)], g.at[pl.ds(to, count)]
        if cols is not None:
            src, dst = src.at[:, :, cols], dst.at[:, :, cols]
        k = len(sends)
        copy = pltpu.make_async_remote_copy(
            src_ref=src, dst_ref=dst, send_sem=gs_sem.at[k], recv_sem=gr_sem.at[k],
            device_id=at(*step), device_id_type=MESH,
        )
        copy.start()
        sends.append(copy)
        return copy

    coming = {}

    def spread(places):
        count = len(places)
        swap = push(places[0], count, (0, 0, 1))
        for _, dz, _ in places:
            coming[0, dz, 1] = swap
        for dx in (1, 3, 2):
            copy = push(places[0], count, ((-dx) % X, 0, 0))
            for _, dz, _ in places:
                coming[dx, dz, 0] = copy

    def await_blocks(places):
        seen = []
        for place in places:
            copy = coming.pop(place, None)
            if copy is not None and all(copy is not other for other in seen):
                copy.wait_recv()
                seen.append(copy)

    def multiply(first, count, width=TILE, after=None):
        def tile(n, carry):
            cols = pl.ds(pl.multiple_of(n * width, width), width)
            left = g[pl.ds(first, count)].reshape(count * ROWS, D)
            logits = jnp.dot(left, w[:, cols], preferred_element_type=jnp.float32)
            sent = jnp.exp((15.0 * CODE) * jnp.tanh(logits * (1.0 / 30.0))).astype(jnp.bfloat16)
            sbuf[pl.ds(first, count), :, cols] = sent.reshape(count, ROWS, width)
            if after is not None:
                after(cols)
            return carry

        lax.fori_loop(0, OWN // width, tile, 0)

    def result(s, to, step, cols=slice(None)):
        return pltpu.make_async_remote_copy(
            src_ref=sbuf.at[s, :, cols], dst_ref=rbuf.at[to, :, cols], send_sem=os_sem.at[s], recv_sem=or_sem.at[to],
            device_id=at(*step), device_id_type=MESH,
        )

    results = []

    def depth(dz):
        part = (dz + 3) // 4
        return part * (2 - part) * (2 * dz - 1) + part * (part - 1) // 2 * (2 * Z - 2 * dz)

    def product(places, last):
        first, count = SLOT[places[0]], len(places)
        pieces = PIECES.get(first, 0)
        if pieces:

            def after(cols):
                for dx, dz, dc in places:
                    result(SLOT[dx, dz, dc], SLOT[(-dx) % X, (-dz) % Z, dc], (dx, dz, dc), cols).start()

            multiply(first, count, OWN // pieces, after)
            results.extend(result(SLOT[p], SLOT[-p[0] % X, -p[1] % Z, p[2]], p) for p in places)
            return
        multiply(first, count)
        if last:
            for target, core in LATE:
                dz, dc = (target - z + Z) % Z, (core + c) % C
                copy = result(first + 8 * dc + depth(dz), first + 8 * dc + depth((Z - dz) % Z), (2, dz, dc))
                copy.start()
                results.append(copy)
            return
        for dx, dz, dc in sorted(places, key=lambda p: (p[2], MIXED.index(p[1]))) if count > 6 else places:
            if (dx, dz, dc) != (0, 0, 0):
                copy = result(SLOT[dx, dz, dc], SLOT[(-dx) % X, (-dz) % Z, dc], (dx, dz, dc))
                copy.start()
                results.append(copy)

    halves = (pl.ds(0, D // 2), pl.ds(D // 2, D // 2))
    down = push((0, 0, 0), 1, (0, 7, 0))
    up = push((0, 0, 0), 1, (0, 1, 0))
    spread([(0, 0, 0)])
    for what, places in PLAN:
        if what == "ring":
            down.wait_recv()
            up.wait_recv()
            k = places[0][1]
            if k < 4:
                down = push((0, k, 0), 1, (0, 7, 0), halves[0] if k == 3 else None)
                up = push((0, Z - k, 0), 1, (0, 1, 0), halves[1] if k == 3 else None)
            spread(places)
        elif what == "swap":
            await_blocks(places)
            copy = push(places[0], len(places), (0, 0, 1))
            for dx, dz, _ in places:
                coming[dx, dz, 1] = copy
        else:
            await_blocks(places)
            while loads:
                loads.pop().wait()
            product(places, what == "last")

    def take(s, buf):
        column = index(*SLOTS[s]) * OWN
        total = acc[...]
        for n in range(0, OWN, 512):
            part = jnp.log(buf[s, :, n : n + 512].astype(jnp.float32)) * (1.0 / CODE)
            scaled[:, pl.ds(pl.multiple_of(column + n, 512), 512)] = part
            terms = jnp.exp(part - 15.0)
            for m in range(0, 512, 128):
                total += terms[:, m : m + 128]
        acc[...] = total

    take(SELF, sbuf)
    for copy in sends:
        copy.wait_send()
    sent = 0
    for s in range(N):
        if s != SELF:
            result(s, s, SLOTS[s]).wait_recv()
            take(s, rbuf)
        if s >= 24 and sent < len(results):
            results[sent].wait_send()
            sent += 1
    total = jnp.sum(acc[...], axis=1, keepdims=True)
    shift[...] = jnp.broadcast_to(15.0 + jnp.log(total), shift.shape)
    for copy in results[sent:]:
        copy.wait_send()


FINISH = 8
WIDTH = N * OWN // FINISH


def finish(scaled, shift, out, buf, sem):
    copies = []
    for i in range(FINISH):
        cols = pl.ds(i * WIDTH, WIDTH)
        buf[:, cols] = (scaled[:, cols] - shift[:, :1]).astype(jnp.bfloat16)
        copies.append(pltpu.make_async_copy(buf.at[:, cols], out.at[:, cols], sem.at[i]))
        copies[-1].start()
    for copy in copies:
        copy.wait()


def local(hidden, norm_gain, head_weight):
    vmem = pl.BlockSpec(memory_space=pltpu.VMEM)
    anywhere = pl.BlockSpec(memory_space=pl.ANY)
    scaled, shift = pl.pallas_call(
        kernel,
        name="gather_head_exchange",
        out_shape=(
            jax.ShapeDtypeStruct((ROWS, N * OWN), jnp.float32),
            jax.ShapeDtypeStruct((ROWS, 128), jnp.float32),
        ),
        in_specs=[vmem, vmem, anywhere],
        out_specs=(vmem, vmem),
        scratch_shapes=[
            pltpu.VMEM((D, OWN), jnp.bfloat16),
            pltpu.VMEM((N, ROWS, D), jnp.bfloat16),
            pltpu.VMEM((N, ROWS, OWN), jnp.bfloat16),
            pltpu.VMEM((N, ROWS, OWN), jnp.bfloat16),
            pltpu.VMEM((ROWS, 128), jnp.float32),
            pltpu.SemaphoreType.DMA((OWN // TILE,)),
            pltpu.SemaphoreType.DMA((N,)),
            pltpu.SemaphoreType.DMA((N,)),
            pltpu.SemaphoreType.DMA((N,)),
            pltpu.SemaphoreType.DMA((N,)),
        ],
        compiler_params=pltpu.CompilerParams(
            collective_id=0, has_side_effects=True, vmem_limit_bytes=42 * 1024 * 1024
        ),
        cost_estimate=pl.CostEstimate(
            flops=2 * N * ROWS * D * OWN, bytes_accessed=18 * 1024 * 1024, transcendentals=4 * N * ROWS * OWN
        ),
    )(hidden, norm_gain, head_weight)
    return pl.pallas_call(
        finish,
        name="finish",
        out_shape=jax.ShapeDtypeStruct((ROWS, N * OWN), jnp.bfloat16),
        in_specs=[vmem, vmem],
        out_specs=anywhere,
        scratch_shapes=[pltpu.VMEM((ROWS, N * OWN), jnp.bfloat16), pltpu.SemaphoreType.DMA((FINISH,))],
        compiler_params=pltpu.CompilerParams(vmem_limit_bytes=24 * 1024 * 1024),
        cost_estimate=pl.CostEstimate(flops=2 * ROWS * N * OWN, bytes_accessed=4 * 1024 * 1024, transcendentals=0),
    )(scaled, shift)


def solution(mesh):
    in_specs = (P(("dp", "vocab"), None), P(), P(None, "vocab"))
    out_specs = P(("dp", "vocab"), None)
    return jax.shard_map(local, mesh=mesh, in_specs=in_specs, out_specs=out_specs, check_vma=False)
```

```python
import jax
import jax.numpy as jnp
from jax import lax
from jax.experimental import pallas as pl
from jax.experimental.pallas import tpu as pltpu
from jax.sharding import PartitionSpec as P

X, Z, C = 4, 8, 2
N = X * Z * C
ROWS = 16
D = 2304
OWN = 2048
CODE = 5.5
MESH = pl.DeviceIdType.MESH
TILE = 1024
MIXED = (1, 7, 4, 2, 6, 3, 5, 0)


def near(k):
    return (k,) if k in (0, 4) else (k, Z - k)


def blocks(dxs, ks, dc):
    return [(dx, dz, dc) for k in ks for dx in dxs for dz in near(k)]


def plan():
    here, sides, far = (0,), (1, 3), (2,)
    steps = [("ring", blocks(here, (1,), 0)), ("product", blocks(here, (1,), 0))]
    steps += [("ring", blocks(here, (2,), 0)), ("product", blocks(here, (1,), 1) + blocks(here, (2,), 0))]
    steps += [("swap", blocks(sides, (0, 1), 0)), ("product", blocks(sides, (0, 1), 0))]
    steps += [("ring", blocks(here, (3,), 0)), ("product", blocks(here, (2,), 1) + blocks(here, (3,), 0))]
    steps += [("swap", blocks(sides, (2,), 0)), ("product", blocks(sides, (0, 1), 1) + blocks(sides, (2,), 0))]
    steps += [("ring", blocks(here, (4,), 0)), ("product", blocks(here, (3,), 1) + blocks(here, (0, 4), 0))]
    steps += [("swap", blocks(sides, (3,), 0)), ("product", blocks(sides, (2,), 1) + blocks(sides, (3,), 0))]
    steps += [("product", blocks(here, (0, 4), 1))]
    steps += [("swap", blocks(sides, (4,), 0)), ("product", blocks(sides, (3,), 1) + blocks(sides, (4,), 0))]
    every = (1, 2, 3, 0, 4)
    steps += [("swap", blocks(far, (0, 1, 2, 3, 4), 0)), ("product", blocks(sides, (4,), 1))]
    steps += [("last", blocks(far, (0, 1, 2, 3, 4), 0) + blocks(far, (0, 1, 2, 3, 4), 1))]
    return steps


LATE = [(0, 1), (1, 0), (3, 1), (2, 0), (5, 1), (6, 0), (4, 1), (7, 0), (0, 0), (1, 1), (3, 0), (2, 1), (5, 0), (6, 1), (4, 0), (7, 1)]
PIECES = {0: 4, 2: 4, 6: 2}
PLAN = plan()
SLOTS = [place for what, places in PLAN if what != "ring" and what != "swap" for place in places]
SLOT = {place: i for i, place in enumerate(SLOTS)}
SELF = SLOT[0, 0, 0]


def kernel(hidden, gain, head, scaled, shift, w, g, sbuf, rbuf, acc, w_sem, gs_sem, gr_sem, os_sem, or_sem):
    v = lax.axis_index("vocab")
    y = lax.axis_index("dp")
    x, z, c = v // (Z * C), (v // C) % Z, v % C

    def index(dx, dz, dc):
        return (((x + dx) % X) * Z + (z + dz) % Z) * C + (c + dc) % C

    def at(dx, dz, dc):
        return (y, index(dx, dz, dc))

    barrier = pltpu.get_barrier_semaphore()
    partners = ((0, 1, 0), (0, 7, 0), (1, 0, 0), (3, 0, 0), (2, 0, 0), (0, 0, 1))
    for step in partners:
        pl.semaphore_signal(barrier, inc=1, device_id=at(*step), device_id_type=MESH)

    loads = []
    for n in range(OWN // TILE):
        cols = pl.ds(n * TILE, TILE)
        loads.append(pltpu.make_async_copy(head.at[:, cols], w.at[:, cols], w_sem.at[n]))
        loads[-1].start()
    wide = hidden[...].astype(jnp.float32)
    power = jnp.mean(wide * wide, axis=1, keepdims=True)
    g[SELF] = (wide * lax.rsqrt(power + 1e-06) * gain[...].reshape(1, D)).astype(jnp.bfloat16)
    acc[...] = jnp.zeros_like(acc)
    pl.semaphore_wait(barrier, len(partners))

    sends = []

    def push(place, count, step, cols=None):
        dx, dz, dc = place
        ex, ez, ec = step
        to = SLOT[(dx - ex) % X, (dz - ez) % Z, (dc + ec) % C]
        for i in range(count):
            px, pz, pc = SLOTS[SLOT[place] + i]
            assert SLOTS[to + i] == ((px - ex) % X, (pz - ez) % Z, (pc + ec) % C)
        src, dst = g.at[pl.ds(SLOT[place], count)], g.at[pl.ds(to, count)]
        if cols is not None:
            src, dst = src.at[:, :, cols], dst.at[:, :, cols]
        k = len(sends)
        copy = pltpu.make_async_remote_copy(
            src_ref=src, dst_ref=dst, send_sem=gs_sem.at[k], recv_sem=gr_sem.at[k],
            device_id=at(*step), device_id_type=MESH,
        )
        copy.start()
        sends.append(copy)
        return copy

    coming = {}

    def spread(places):
        count = len(places)
        swap = push(places[0], count, (0, 0, 1))
        for _, dz, _ in places:
            coming[0, dz, 1] = swap
        for dx in (1, 3, 2):
            copy = push(places[0], count, ((-dx) % X, 0, 0))
            for _, dz, _ in places:
                coming[dx, dz, 0] = copy

    def await_blocks(places):
        seen = []
        for place in places:
            copy = coming.pop(place, None)
            if copy is not None and all(copy is not other for other in seen):
                copy.wait_recv()
                seen.append(copy)

    def multiply(first, count, width=TILE, after=None):
        def tile(n, carry):
            cols = pl.ds(pl.multiple_of(n * width, width), width)
            left = g[pl.ds(first, count)].reshape(count * ROWS, D)
            logits = jnp.dot(left, w[:, cols], preferred_element_type=jnp.float32)
            sent = jnp.exp((15.0 * CODE) * jnp.tanh(logits * (1.0 / 30.0))).astype(jnp.bfloat16)
            sbuf[pl.ds(first, count), :, cols] = sent.reshape(count, ROWS, width)
            if after is not None:
                after(cols)
            return carry

        lax.fori_loop(0, OWN // width, tile, 0)

    def result(s, to, step, cols=slice(None)):
        return pltpu.make_async_remote_copy(
            src_ref=sbuf.at[s, :, cols], dst_ref=rbuf.at[to, :, cols], send_sem=os_sem.at[s], recv_sem=or_sem.at[to],
            device_id=at(*step), device_id_type=MESH,
        )

    results = []

    def depth(dz):
        part = (dz + 3) // 4
        return part * (2 - part) * (2 * dz - 1) + part * (part - 1) // 2 * (2 * Z - 2 * dz)

    def product(places, last):
        first, count = SLOT[places[0]], len(places)
        pieces = PIECES.get(first, 0)
        if pieces:

            def after(cols):
                for dx, dz, dc in places:
                    result(SLOT[dx, dz, dc], SLOT[(-dx) % X, (-dz) % Z, dc], (dx, dz, dc), cols).start()

            multiply(first, count, OWN // pieces, after)
            results.extend(result(SLOT[p], SLOT[-p[0] % X, -p[1] % Z, p[2]], p) for p in places)
            return
        multiply(first, count)
        if last:
            for target, core in LATE:
                dz, dc = (target - z + Z) % Z, (core + c) % C
                copy = result(first + 8 * dc + depth(dz), first + 8 * dc + depth((Z - dz) % Z), (2, dz, dc))
                copy.start()
                results.append(copy)
            return
        for dx, dz, dc in sorted(places, key=lambda p: (p[2], MIXED.index(p[1]))) if count > 6 else places:
            if (dx, dz, dc) != (0, 0, 0):
                copy = result(SLOT[dx, dz, dc], SLOT[(-dx) % X, (-dz) % Z, dc], (dx, dz, dc))
                copy.start()
                results.append(copy)

    halves = (pl.ds(0, D // 2), pl.ds(D // 2, D // 2))
    down = push((0, 0, 0), 1, (0, 7, 0))
    up = push((0, 0, 0), 1, (0, 1, 0))
    spread([(0, 0, 0)])
    for what, places in PLAN:
        if what == "ring":
            down.wait_recv()
            up.wait_recv()
            k = places[0][1]
            if k < 4:
                down = push((0, k, 0), 1, (0, 7, 0), halves[0] if k == 3 else None)
                up = push((0, Z - k, 0), 1, (0, 1, 0), halves[1] if k == 3 else None)
            spread(places)
        elif what == "swap":
            await_blocks(places)
            copy = push(places[0], len(places), (0, 0, 1))
            for dx, dz, _ in places:
                coming[dx, dz, 1] = copy
        else:
            await_blocks(places)
            while loads:
                loads.pop().wait()
            product(places, what == "last")

    def take(s, buf):
        column = index(*SLOTS[s]) * OWN
        total = acc[...]
        for n in range(0, OWN, 512):
            part = jnp.log(buf[s, :, n : n + 512].astype(jnp.float32)) * (1.0 / CODE)
            scaled[:, pl.ds(pl.multiple_of(column + n, 512), 512)] = part
            terms = jnp.exp(part - 15.0)
            for m in range(0, 512, 128):
                total += terms[:, m : m + 128]
        acc[...] = total

    take(SELF, sbuf)
    for copy in sends:
        copy.wait_send()
    sent = 0
    for s in range(N):
        if s != SELF:
            result(s, s, SLOTS[s]).wait_recv()
            take(s, rbuf)
        if s >= 24 and sent < len(results):
            results[sent].wait_send()
            sent += 1
    total = jnp.sum(acc[...], axis=1, keepdims=True)
    shift[...] = jnp.broadcast_to(15.0 + jnp.log(total), shift.shape)
    for copy in results[sent:]:
        copy.wait_send()


FINISH = 8
WIDTH = N * OWN // FINISH


def finish(scaled, shift, out, buf, sem):
    copies = []
    for i in range(FINISH):
        cols = pl.ds(i * WIDTH, WIDTH)
        buf[:, cols] = (scaled[:, cols] - shift[:, :1]).astype(jnp.bfloat16)
        copies.append(pltpu.make_async_copy(buf.at[:, cols], out.at[:, cols], sem.at[i]))
        copies[-1].start()
    for copy in copies:
        copy.wait()


def local(hidden, norm_gain, head_weight):
    vmem = pl.BlockSpec(memory_space=pltpu.VMEM)
    anywhere = pl.BlockSpec(memory_space=pl.ANY)
    scaled, shift = pl.pallas_call(
        kernel,
        name="gather_head_exchange",
        out_shape=(
            jax.ShapeDtypeStruct((ROWS, N * OWN), jnp.float32),
            jax.ShapeDtypeStruct((ROWS, 128), jnp.float32),
        ),
        in_specs=[vmem, vmem, anywhere],
        out_specs=(vmem, vmem),
        scratch_shapes=[
            pltpu.VMEM((D, OWN), jnp.bfloat16),
            pltpu.VMEM((N, ROWS, D), jnp.bfloat16),
            pltpu.VMEM((N, ROWS, OWN), jnp.bfloat16),
            pltpu.VMEM((N, ROWS, OWN), jnp.bfloat16),
            pltpu.VMEM((ROWS, 128), jnp.float32),
            pltpu.SemaphoreType.DMA((OWN // TILE,)),
            pltpu.SemaphoreType.DMA((N,)),
            pltpu.SemaphoreType.DMA((N,)),
            pltpu.SemaphoreType.DMA((N,)),
            pltpu.SemaphoreType.DMA((N,)),
        ],
        compiler_params=pltpu.CompilerParams(
            collective_id=0, has_side_effects=True, vmem_limit_bytes=42 * 1024 * 1024
        ),
        cost_estimate=pl.CostEstimate(
            flops=2 * N * ROWS * D * OWN, bytes_accessed=18 * 1024 * 1024, transcendentals=4 * N * ROWS * OWN
        ),
    )(hidden, norm_gain, head_weight)
    return pl.pallas_call(
        finish,
        name="finish",
        out_shape=jax.ShapeDtypeStruct((ROWS, N * OWN), jnp.bfloat16),
        in_specs=[vmem, vmem],
        out_specs=anywhere,
        scratch_shapes=[pltpu.VMEM((ROWS, N * OWN), jnp.bfloat16), pltpu.SemaphoreType.DMA((FINISH,))],
        compiler_params=pltpu.CompilerParams(vmem_limit_bytes=24 * 1024 * 1024),
        cost_estimate=pl.CostEstimate(flops=2 * ROWS * N * OWN, bytes_accessed=4 * 1024 * 1024, transcendentals=0),
    )(scaled, shift)


def solution(mesh):
    in_specs = (P(("dp", "vocab"), None), P(), P(None, "vocab"))
    out_specs = P(("dp", "vocab"), None)
    return jax.shard_map(local, mesh=mesh, in_specs=in_specs, out_specs=out_specs, check_vma=False)
```

```python
import jax
import jax.numpy as jnp
from jax import lax
from jax.experimental import pallas as pl
from jax.experimental.pallas import tpu as pltpu
from jax.sharding import PartitionSpec as P

X, Z, C = 4, 8, 2
N = X * Z * C
ROWS = 16
D = 2304
OWN = 2048
CODE = 5.5
MESH = pl.DeviceIdType.MESH
TILE = 1024
MIXED = (1, 7, 4, 2, 6, 3, 5, 0)


def near(k):
    return (k,) if k in (0, 4) else (k, Z - k)


def blocks(dxs, ks, dc):
    return [(dx, dz, dc) for k in ks for dx in dxs for dz in near(k)]


def plan():
    here, sides, far = (0,), (1, 3), (2,)
    steps = [("ring", blocks(here, (1,), 0)), ("product", blocks(here, (1,), 0))]
    steps += [("ring", blocks(here, (2,), 0)), ("product", blocks(here, (1,), 1) + blocks(here, (2,), 0))]
    steps += [("swap", blocks(sides, (0, 1), 0)), ("product", blocks(sides, (0, 1), 0))]
    steps += [("ring", blocks(here, (3,), 0)), ("product", blocks(here, (2,), 1) + blocks(here, (3,), 0))]
    steps += [("swap", blocks(sides, (2,), 0)), ("product", blocks(sides, (0, 1), 1) + blocks(sides, (2,), 0))]
    steps += [("ring", blocks(here, (4,), 0)), ("product", blocks(here, (3,), 1) + blocks(here, (0, 4), 0))]
    steps += [("swap", blocks(sides, (3,), 0)), ("product", blocks(sides, (2,), 1) + blocks(sides, (3,), 0))]
    steps += [("product", blocks(here, (0, 4), 1))]
    steps += [("swap", blocks(sides, (4,), 0)), ("product", blocks(sides, (3,), 1) + blocks(sides, (4,), 0))]
    every = (1, 2, 3, 0, 4)
    steps += [("swap", blocks(far, (0, 1, 2, 3, 4), 0)), ("product", blocks(sides, (4,), 1))]
    steps += [("last", blocks(far, (0, 1, 2, 3, 4), 0) + blocks(far, (0, 1, 2, 3, 4), 1))]
    return steps


LATE = [(0, 1), (1, 0), (3, 1), (2, 0), (5, 1), (6, 0), (4, 1), (7, 0), (0, 0), (1, 1), (3, 0), (2, 1), (5, 0), (6, 1), (4, 0), (7, 1)]
PIECES = {0: 4, 2: 4, 6: 2}
PLAN = plan()
SLOTS = [place for what, places in PLAN if what != "ring" and what != "swap" for place in places]
SLOT = {place: i for i, place in enumerate(SLOTS)}
SELF = SLOT[0, 0, 0]


def kernel(hidden, gain, head, scaled, shift, w, g, sbuf, rbuf, acc, w_sem, gs_sem, gr_sem, os_sem, or_sem):
    v = lax.axis_index("vocab")
    y = lax.axis_index("dp")
    x, z, c = v // (Z * C), (v // C) % Z, v % C

    def index(dx, dz, dc):
        return (((x + dx) % X) * Z + (z + dz) % Z) * C + (c + dc) % C

    def at(dx, dz, dc):
        return (y, index(dx, dz, dc))

    barrier = pltpu.get_barrier_semaphore()
    partners = ((0, 1, 0), (0, 7, 0), (1, 0, 0), (3, 0, 0), (2, 0, 0), (0, 0, 1))
    for step in partners:
        pl.semaphore_signal(barrier, inc=1, device_id=at(*step), device_id_type=MESH)

    loads = []
    for n in range(OWN // TILE):
        cols = pl.ds(n * TILE, TILE)
        loads.append(pltpu.make_async_copy(head.at[:, cols], w.at[:, cols], w_sem.at[n]))
        loads[-1].start()
    wide = hidden[...].astype(jnp.float32)
    power = jnp.mean(wide * wide, axis=1, keepdims=True)
    g[SELF] = (wide * lax.rsqrt(power + 1e-06) * gain[...].reshape(1, D)).astype(jnp.bfloat16)
    acc[...] = jnp.zeros_like(acc)
    pl.semaphore_wait(barrier, len(partners))

    sends = []

    def push(place, count, step, cols=None):
        dx, dz, dc = place
        ex, ez, ec = step
        to = SLOT[(dx - ex) % X, (dz - ez) % Z, (dc + ec) % C]
        for i in range(count):
            px, pz, pc = SLOTS[SLOT[place] + i]
            assert SLOTS[to + i] == ((px - ex) % X, (pz - ez) % Z, (pc + ec) % C)
        src, dst = g.at[pl.ds(SLOT[place], count)], g.at[pl.ds(to, count)]
        if cols is not None:
            src, dst = src.at[:, :, cols], dst.at[:, :, cols]
        k = len(sends)
        copy = pltpu.make_async_remote_copy(
            src_ref=src, dst_ref=dst, send_sem=gs_sem.at[k], recv_sem=gr_sem.at[k],
            device_id=at(*step), device_id_type=MESH,
        )
        copy.start()
        sends.append(copy)
        return copy

    coming = {}

    def spread(places):
        count = len(places)
        swap = push(places[0], count, (0, 0, 1))
        for _, dz, _ in places:
            coming[0, dz, 1] = swap

    def sideways(places):
        count = len(places)
        for dx in (1, 3, 2):
            copy = push(places[0], count, ((-dx) % X, 0, 0))
            for _, dz, _ in places:
                coming[dx, dz, 0] = copy

    def await_blocks(places):
        seen = []
        for place in places:
            copy = coming.pop(place, None)
            if copy is not None and all(copy is not other for other in seen):
                copy.wait_recv()
                seen.append(copy)

    def multiply(first, count, width=TILE, after=None):
        def tile(n, carry):
            cols = pl.ds(pl.multiple_of(n * width, width), width)
            left = g[pl.ds(first, count)].reshape(count * ROWS, D)
            logits = jnp.dot(left, w[:, cols], preferred_element_type=jnp.float32)
            sent = jnp.exp((15.0 * CODE) * jnp.tanh(logits * (1.0 / 30.0))).astype(jnp.bfloat16)
            sbuf[pl.ds(first, count), :, cols] = sent.reshape(count, ROWS, width)
            if after is not None:
                after(cols)
            return carry

        lax.fori_loop(0, OWN // width, tile, 0)

    def result(s, to, step, cols=slice(None)):
        return pltpu.make_async_remote_copy(
            src_ref=sbuf.at[s, :, cols], dst_ref=rbuf.at[to, :, cols], send_sem=os_sem.at[s], recv_sem=or_sem.at[to],
            device_id=at(*step), device_id_type=MESH,
        )

    results = []

    def depth(dz):
        part = (dz + 3) // 4
        return part * (2 - part) * (2 * dz - 1) + part * (part - 1) // 2 * (2 * Z - 2 * dz)

    def product(places, last):
        first, count = SLOT[places[0]], len(places)
        pieces = PIECES.get(first, 0)
        if pieces:

            def after(cols):
                for dx, dz, dc in places:
                    result(SLOT[dx, dz, dc], SLOT[(-dx) % X, (-dz) % Z, dc], (dx, dz, dc), cols).start()

            multiply(first, count, OWN // pieces, after)
            results.extend(result(SLOT[p], SLOT[-p[0] % X, -p[1] % Z, p[2]], p) for p in places)
            return
        multiply(first, count)
        if last:
            for target, core in LATE:
                dz, dc = (target - z + Z) % Z, (core + c) % C
                copy = result(first + 8 * dc + depth(dz), first + 8 * dc + depth((Z - dz) % Z), (2, dz, dc))
                copy.start()
                results.append(copy)
            return
        for dx, dz, dc in sorted(places, key=lambda p: (p[2], MIXED.index(p[1]))) if count > 6 else places:
            if (dx, dz, dc) != (0, 0, 0):
                copy = result(SLOT[dx, dz, dc], SLOT[(-dx) % X, (-dz) % Z, dc], (dx, dz, dc))
                copy.start()
                results.append(copy)

    halves = (pl.ds(0, D // 2), pl.ds(D // 2, D // 2))
    down = push((0, 0, 0), 1, (0, 7, 0))
    up = push((0, 0, 0), 1, (0, 1, 0))
    spread([(0, 0, 0)])
    sideways([(0, 0, 0)])
    held_back = []
    for what, places in PLAN:
        if what == "ring":
            down.wait_recv()
            up.wait_recv()
            k = places[0][1]
            if k < 4:
                down = push((0, k, 0), 1, (0, 7, 0), halves[0] if k == 3 else None)
                up = push((0, Z - k, 0), 1, (0, 1, 0), halves[1] if k == 3 else None)
            spread(places)
            held_back.append(places)
        elif what == "swap":
            await_blocks(places)
            copy = push(places[0], len(places), (0, 0, 1))
            for dx, dz, _ in places:
                coming[dx, dz, 1] = copy
        else:
            await_blocks(places)
            while loads:
                loads.pop().wait()
            product(places, what == "last")
            while held_back:
                sideways(held_back.pop())

    def take(s, buf):
        column = index(*SLOTS[s]) * OWN
        total = acc[...]
        for n in range(0, OWN, 512):
            part = jnp.log(buf[s, :, n : n + 512].astype(jnp.float32)) * (1.0 / CODE)
            scaled[:, pl.ds(pl.multiple_of(column + n, 512), 512)] = part
            terms = jnp.exp(part - 15.0)
            for m in range(0, 512, 128):
                total += terms[:, m : m + 128]
        acc[...] = total

    take(SELF, sbuf)
    for copy in sends:
        copy.wait_send()
    sent = 0
    for s in range(N):
        if s != SELF:
            result(s, s, SLOTS[s]).wait_recv()
            take(s, rbuf)
        if s >= 24 and sent < len(results):
            results[sent].wait_send()
            sent += 1
    total = jnp.sum(acc[...], axis=1, keepdims=True)
    shift[...] = jnp.broadcast_to(15.0 + jnp.log(total), shift.shape)
    for copy in results[sent:]:
        copy.wait_send()


FINISH = 8
WIDTH = N * OWN // FINISH


def finish(scaled, shift, out, buf, sem):
    copies = []
    for i in range(FINISH):
        cols = pl.ds(i * WIDTH, WIDTH)
        buf[:, cols] = (scaled[:, cols] - shift[:, :1]).astype(jnp.bfloat16)
        copies.append(pltpu.make_async_copy(buf.at[:, cols], out.at[:, cols], sem.at[i]))
        copies[-1].start()
    for copy in copies:
        copy.wait()


def local(hidden, norm_gain, head_weight):
    vmem = pl.BlockSpec(memory_space=pltpu.VMEM)
    anywhere = pl.BlockSpec(memory_space=pl.ANY)
    scaled, shift = pl.pallas_call(
        kernel,
        name="gather_head_exchange",
        out_shape=(
            jax.ShapeDtypeStruct((ROWS, N * OWN), jnp.float32),
            jax.ShapeDtypeStruct((ROWS, 128), jnp.float32),
        ),
        in_specs=[vmem, vmem, anywhere],
        out_specs=(vmem, vmem),
        scratch_shapes=[
            pltpu.VMEM((D, OWN), jnp.bfloat16),
            pltpu.VMEM((N, ROWS, D), jnp.bfloat16),
            pltpu.VMEM((N, ROWS, OWN), jnp.bfloat16),
            pltpu.VMEM((N, ROWS, OWN), jnp.bfloat16),
            pltpu.VMEM((ROWS, 128), jnp.float32),
            pltpu.SemaphoreType.DMA((OWN // TILE,)),
            pltpu.SemaphoreType.DMA((N,)),
            pltpu.SemaphoreType.DMA((N,)),
            pltpu.SemaphoreType.DMA((N,)),
            pltpu.SemaphoreType.DMA((N,)),
        ],
        compiler_params=pltpu.CompilerParams(
            collective_id=0, has_side_effects=True, vmem_limit_bytes=42 * 1024 * 1024
        ),
        cost_estimate=pl.CostEstimate(
            flops=2 * N * ROWS * D * OWN, bytes_accessed=18 * 1024 * 1024, transcendentals=4 * N * ROWS * OWN
        ),
    )(hidden, norm_gain, head_weight)
    return pl.pallas_call(
        finish,
        name="finish",
        out_shape=jax.ShapeDtypeStruct((ROWS, N * OWN), jnp.bfloat16),
        in_specs=[vmem, vmem],
        out_specs=anywhere,
        scratch_shapes=[pltpu.VMEM((ROWS, N * OWN), jnp.bfloat16), pltpu.SemaphoreType.DMA((FINISH,))],
        compiler_params=pltpu.CompilerParams(vmem_limit_bytes=24 * 1024 * 1024),
        cost_estimate=pl.CostEstimate(flops=2 * ROWS * N * OWN, bytes_accessed=4 * 1024 * 1024, transcendentals=0),
    )(scaled, shift)


def solution(mesh):
    in_specs = (P(("dp", "vocab"), None), P(), P(None, "vocab"))
    out_specs = P(("dp", "vocab"), None)
    return jax.shard_map(local, mesh=mesh, in_specs=in_specs, out_specs=out_specs, check_vma=False)
```
